768 devices in a mesh: fsdp: 128 (over y, x, z_hi, core), tensor: 6 (over z_lo).
Axes of the slice: x: 4, y: 8, z: 12 (z_hi: 2, z_lo: 6; z = z_hi * 6 + z_lo), core: 2. Of those that a mesh axis runs over, the one named last changes fastest.
Arguments:
- queries: bfloat16 [16384, 3072], P('fsdp', 'tensor'), may hold values from -6 to 6
- keys: bfloat16 [16384, 3072], P('fsdp', 'tensor'), may hold values from -6 to 6
- values: bfloat16 [16384, 3072], P('fsdp', 'tensor'), may hold values from -6 to 6
- out_weight: bfloat16 [3072, 6144], P('tensor', 'fsdp'), may hold values from -0.5 to 0.5
- cotangent: bfloat16 [16384, 6144], P('fsdp', 'tensor'), may hold values from -6 to 6
- image_ids: int32 [128, 128], P('fsdp'), may hold values from 0 to 7, never falling along the last dimension, each value on 1 to 64 neighbouring positions
Outputs:
- projected: bfloat16 [16384, 6144], P('fsdp', 'tensor')
- grad_queries: bfloat16 [16384, 3072], P('fsdp', 'tensor')
- grad_keys: bfloat16 [16384, 3072], P('fsdp', 'tensor')
- grad_values: bfloat16 [16384, 3072], P('fsdp', 'tensor')
The draws below stay inside these ranges and needn't reach their ends.
Inputs may be any that keep to these rules, and one draw needn't show every extreme that they name: `image_ids`: 8 images on each fsdp index, numbered in order; the largest has exactly 64 patches.
All inputs are finite; a program needn't handle non-finite values.
Results may differ from the reference program's by a relative error of at most 0.015.
Values may be sent and summed in bfloat16 or wider, within the bound.
A program may use at most 32 MiB of HBM per device.

```python
import math
import jax
import jax.numpy as jnp
import numpy as np
from jax import lax

D = 6144
HEADS = 24
HD = 128
TOK_DEV = 128
IMG_DEV = 8
IMG_MOST = 64
TOKENS = 16384
N_FSDP = 128
N_TENSOR = 6


def draw_queries(key, part):
    key = jax.random.fold_in(key, 5)
    base = jax.random.normal(key, (TOKENS, HEADS * HD), jnp.float32)
    return jnp.clip(base, -6.0, 6.0).astype(jnp.bfloat16)


def draw_keys(key, part):
    key = jax.random.fold_in(key, 9)
    base = jax.random.normal(key, (TOKENS, HEADS * HD), jnp.float32)
    return jnp.clip(base, -6.0, 6.0).astype(jnp.bfloat16)


def levels(own_key, shape, shards, low, largest):
    gain = 1.0
    for dim, shards_of in shards:
        draws = jax.random.uniform(jax.random.fold_in(jax.random.fold_in(own_key, 6), dim), (shards_of,), jnp.float32, low / len(shards), largest / len(shards))
        gain = gain * jnp.repeat(jnp.exp(draws), shape[dim] // shards_of).reshape((-1,) + (1,) * (len(shape) - 1 - dim))
    return gain


def split_up(count, total, bound, slope):
    loads = [(1 << 20) // math.isqrt(standing ** slope) + 1 for standing in range(2, count + 1)]
    surplus, given = total - bound - (count - 1), [1] * (count - 1)
    while surplus > 0:
        free = [i for i in range(count - 1) if given[i] < bound]
        pool, remaining = sum([loads[i] for i in free]), surplus
        for i in free:
            more = min(bound - given[i], max(1, remaining * loads[i] // pool), surplus)
            given[i] = given[i] + more
            surplus = surplus - more
    return np.array([bound] + given)


def uneven_parts(stream_key, number_of, total, limit, slope):
    if number_of == 2:
        one = jax.random.randint(stream_key, (), max(1, total - limit), min(limit, total - 1) + 1)
        return jnp.stack([one, total - one])
    tallies = jnp.asarray(split_up(number_of, total, limit, slope), jnp.int32)
    twos = (number_of - 1) // 2
    source_of, sink = tallies[1:1 + 2 * twos:2], tallies[2:2 + 2 * twos:2]
    margin = jnp.minimum(source_of - 1, limit - sink)
    shifted = jax.random.randint(jax.random.fold_in(stream_key, 1), (twos,), 0, 1 << 20) % (margin + 1)
    tallies = tallies.at[1:1 + 2 * twos:2].set(source_of - shifted).at[2:2 + 2 * twos:2].set(sink + shifted)
    return tallies[jax.random.permutation(jax.random.fold_in(stream_key, 2), number_of)]


def normal_values(own_key, shape, deviation, reach, shards=(), dtype=jnp.bfloat16):
    drawn = jax.random.normal(own_key, shape, jnp.float32) * deviation
    if len(shards) > 0:
        drawn = levels(own_key, shape, shards, -0.22, 0.18) * drawn
    return jnp.clip(drawn, min=-reach, max=reach).astype(dtype)


def setup_inputs(seed: int = 0) -> dict:
    arg_keys = jax.random.split(jax.random.key(seed), 7)
    return {
        "queries": draw_queries(jax.random.fold_in(arg_keys[6], 71), 0),
        "keys": draw_keys(jax.random.fold_in(arg_keys[6], 71), 0),
        "values": normal_values(arg_keys[2], (TOKENS, HEADS * HD), 1.0, 6.0, ((0, 128), (1, 6))),
        "out_weight": normal_values(arg_keys[3], (HEADS * HD, D), HD ** -0.5, 0.5, ((0, 6), (1, 128))),
        "cotangent": normal_values(arg_keys[4], (TOKENS, D), 1.0, 6.0, ((0, 128), (1, 6))),
        "image_ids": jax.vmap(lambda own: jnp.searchsorted(jnp.cumsum(uneven_parts(own, IMG_DEV, TOK_DEV, IMG_MOST, 2)), jnp.arange(TOK_DEV), side="right"))(jax.random.split(arg_keys[5], N_FSDP)).reshape((N_FSDP, TOK_DEV)).astype(jnp.int32),
    }


def attend_forward(query, key, value, same):
    scores = jnp.dot(query, key.T, preferred_element_type=jnp.float32) * (HD ** -0.5)
    scores = jnp.where(same, scores, -1e30)
    top = jnp.max(scores, axis=-1, keepdims=True)
    weights = jnp.exp(scores - top)
    probs = weights / jnp.sum(weights, axis=-1, keepdims=True)
    probs_low = probs.astype(jnp.bfloat16)
    attended = jnp.dot(probs_low, value, preferred_element_type=jnp.float32).astype(jnp.bfloat16)
    return attended, probs


def attend_backward(query, key, value, probs, grad_out):
    probs_low = probs.astype(jnp.bfloat16)
    grad_value = jnp.dot(probs_low.T, grad_out, preferred_element_type=jnp.float32).astype(jnp.bfloat16)
    grad_probs = jnp.dot(grad_out, value.T, preferred_element_type=jnp.float32)
    delta = jnp.sum(grad_probs * probs, axis=-1, keepdims=True)
    grad_scores = (probs * (grad_probs - delta) * (HD ** -0.5)).astype(jnp.bfloat16)
    grad_query = jnp.dot(grad_scores, key, preferred_element_type=jnp.float32).astype(jnp.bfloat16)
    grad_key = jnp.dot(grad_scores.T, query, preferred_element_type=jnp.float32).astype(jnp.bfloat16)
    return grad_query, grad_key, grad_value


def reference(queries, keys, values, out_weight, cotangent, image_ids):
    grad_attended = jnp.dot(cotangent, out_weight.T, preferred_element_type=jnp.float32).astype(jnp.bfloat16)

    def one_shard(pieces):
        query, key, value, grad_out, ids = pieces
        same = ids[:, None] == ids[None, :]
        outs_att, outs_q, outs_k, outs_v = [], [], [], []
        for head in range(HEADS):
            lo = head * HD
            hi = lo + HD
            attended, probs = attend_forward(query[:, lo:hi], key[:, lo:hi], value[:, lo:hi], same)
            grad_q, grad_k, grad_v = attend_backward(query[:, lo:hi], key[:, lo:hi], value[:, lo:hi], probs, grad_out[:, lo:hi])
            outs_att.append(attended)
            outs_q.append(grad_q)
            outs_k.append(grad_k)
            outs_v.append(grad_v)
        joined = lambda items: jnp.concatenate(items, axis=1)
        return joined(outs_att), joined(outs_q), joined(outs_k), joined(outs_v)

    rows = lambda a: a.reshape(N_FSDP, TOK_DEV, HEADS * HD)
    attended, grad_q, grad_k, grad_v = lax.map(
        one_shard, (rows(queries), rows(keys), rows(values), rows(grad_attended), image_ids))
    flat = lambda a: a.reshape(TOKENS, HEADS * HD)
    flat_attended = flat(attended)
    group = HEADS * HD // N_TENSOR
    total = jnp.zeros((TOKENS, D), jnp.float32)
    for index in range(N_TENSOR):
        cols = flat_attended[:, index * group:(index + 1) * group]
        wrows = out_weight[index * group:(index + 1) * group, :]
        partial_value = jnp.dot(cols, wrows, preferred_element_type=jnp.float32).astype(jnp.bfloat16)
        partial_value = lax.optimization_barrier(partial_value)
        total = total + partial_value.astype(jnp.float32)
    projected = total.astype(jnp.bfloat16)
    return projected, flat(grad_q), flat(grad_k), flat(grad_v)
```

```python
import functools

import jax
import jax.numpy as jnp
from jax import lax
from jax.experimental import pallas as pl
from jax.experimental.pallas import tpu as pltpu
from jax.sharding import PartitionSpec as P

HD = 128
SCALE = HD ** (-0.5)
MESH = pl.DeviceIdType.MESH
NX, NY, NT = 4, 8, 6
UNIT = 16
F32 = jnp.float32
BF16 = jnp.bfloat16

NT_DIMS = (((1,), (1,)), ((), ()))
TN_DIMS = (((0,), (0,)), ((), ()))


def mod(a, n):
    return lax.rem(a + 4 * n, n)


def shift_of(slab):
    a = (slab * (5 - slab)) // 2
    m = a // 2 + a // 3
    return 3 - 5 * m + 2 * m * m


def coords(f):
    return f // 16, (f // 4) % 4, (f // 2) % 2, f % 2


def index_of(y, x, zh, c):
    return ((y * NX + x) * 2 + zh) * 2 + c


class Ring:
    def __init__(self, n, pos, device, region, send_sem, recv_sem):
        self.n, self.pos, self.device, self.region = n, pos, device, region
        self.send_sem, self.recv_sem = send_sem, recv_sem
        self.steps = n // 2

    def copy(self, d, k, origin):
        last = k == self.steps - 1
        ref = self.region(origin, d if last else None)
        i = d * self.steps + k
        return pltpu.make_async_remote_copy(
            src_ref=ref, dst_ref=ref,
            send_sem=self.send_sem(i), recv_sem=self.recv_sem(i),
            device_id=self.device(1 if d == 0 else -1), device_id_type=MESH,
        )

    def origin(self, d, k):
        return mod(self.pos - k if d == 0 else self.pos + k, self.n)

    def send(self, k):
        for d in (0, 1):
            self.copy(d, k, self.origin(d, k)).start()

    def wait(self, k):
        for d in (0, 1):
            self.copy(d, k, self.origin(d, k + 1)).wait_recv()

    def finish(self):
        for k in range(self.steps):
            for d in (0, 1):
                self.copy(d, k, self.origin(d, k)).wait_send()


def kernel(q_ref, k_ref, v_ref, wt_ref, cot_ref, ids_ref,
           proj_ref, gq_ref, gk_ref, gv_ref,
           slab, att, fr_l, fr_r, snd, part, probs,
           pre_s, pre_r, ax_s, ax_r, by_s, by_r, ay_s, ay_r, bx_s, bx_r,
           dd_s, dd_r, zr_s, zl_s, za_r, rs_s, rl_r, rr_r):
    f = lax.axis_index("fsdp")
    t = lax.axis_index("tensor")
    y, x, zh, c = coords(f)
    turn = shift_of(t)
    y2 = lax.rem(y + turn, NY)
    in_a = t // 3

    sib = f + 1 - 2 * c
    x_dev = lambda s: (index_of(y, mod(x + s, NX), zh, c), t)
    y_dev = lambda s: (index_of(mod(y + s, NY), x, zh, c), t)

    barrier = pltpu.get_barrier_semaphore()

    def greet(device):
        pl.semaphore_signal(barrier, inc=1, device_id=device, device_id_type=MESH)

    for j in range(NT):
        v = c * 32 + (y2 * 4 + x if j >= 3 else x * 8 + y2)
        greet(((64 * t + v) // 3, j))
    for s in (1, -1):
        greet(x_dev(s))
        greet(y_dev(s))
    greet((sib, t))

    @pl.when(t > 0)
    def _():
        greet((f, t - 1))

    @pl.when(t < NT - 1)
    def _():
        greet((f, t + 1))

    pl.semaphore_wait(barrier, 6 + 5 + (t + NT - 1) // NT + (2 * NT - 2 - t) // NT)

    def pre_copy(i, z):
        u = 3 * f + i
        to = u // 64
        v = u % 64
        rest = v % 32
        ya, xa = rest // 4, rest % 4
        yb, xb = rest % 8, rest // 8
        yy = in_a * ya + (1 - in_a) * yb
        xx = in_a * xa + (1 - in_a) * xb
        yd = lax.rem(yy - shift_of(to) + NY, NY)
        return pltpu.make_async_remote_copy(
            src_ref=wt_ref.at[pl.ds(i * UNIT, UNIT), :],
            dst_ref=slab.at[t, pl.ds(pl.multiple_of(v * UNIT, UNIT), UNIT), :],
            send_sem=pre_s.at[2 * i + z], recv_sem=pre_r.at[t],
            device_id=(index_of(yd, xx, z, v // 32), to), device_id_type=MESH,
        )

    for i in range(3):
        for z in (0, 1):
            pre_copy(i, z).start()

    ids_row = jnp.broadcast_to(ids_ref[...].astype(F32), (HD, HD))
    same = ids_row == ids_row.T
    for h in range(4):
        cols = slice(h * HD, (h + 1) * HD)
        s = lax.dot_general(q_ref[:, cols], k_ref[:, cols], NT_DIMS, preferred_element_type=F32) * SCALE
        s = jnp.where(same, s, -1e30)
        w = jnp.exp(s - jnp.max(s, axis=-1, keepdims=True))
        p = w / jnp.sum(w, axis=-1, keepdims=True)
        probs[h] = p
        a = jnp.dot(p.astype(BF16), v_ref[:, cols], preferred_element_type=F32)
        att[t, :, cols] = a.astype(BF16)

    def att_copy(block, s, k):
        return pltpu.make_async_remote_copy(
            src_ref=att.at[block], dst_ref=att.at[block],
            send_sem=(zr_s if s > 0 else zl_s).at[k], recv_sem=za_r.at[block],
            device_id=(f, t + s), device_id_type=MESH,
        )

    def att_wait(block):
        pltpu.make_async_remote_copy(
            src_ref=att.at[block], dst_ref=att.at[block],
            send_sem=zr_s.at[0], recv_sem=za_r.at[block],
            device_id=(f, t), device_id_type=MESH,
        ).wait_recv()

    def att_step(k):
        for s in (1, -1):
            block = t - s * k
            has = (t >= k) if s > 0 else (t + k <= NT - 1)
            room = (t < NT - 1) if s > 0 else (t > 0)
            if k > 0:
                @pl.when(has)
                def _():
                    att_wait(block)
            if k < NT - 1:
                @pl.when(has & room)
                def _():
                    att_copy(block, s, k).start()

    att_step(0)

    def rows_a(o, whole):
        base = c * 512 + (o if whole else y2) * 64
        return base if whole else base + o * UNIT

    def small_a(o, half):
        r = pl.ds(pl.multiple_of(c * 512 + y2 * 64 + o * UNIT, UNIT), UNIT)
        w = slice(None) if half is None else pl.ds(half * 256, 256)
        return slab.at[pl.ds(3, 3), r, w]

    def small_b(o, half):
        r = pl.ds(pl.multiple_of(c * 512 + x * 128 + lax.rem(o + turn, NY) * UNIT, UNIT), UNIT)
        w = slice(None) if half is None else pl.ds(half * 256, 256)
        return slab.at[pl.ds(0, 3), r, w]

    def big_a(j, o, half):
        r = pl.ds(pl.multiple_of(c * 512 + lax.rem(o + turn, NY) * 64, 64), 64)
        w = slice(None) if half is None else pl.ds(half * 256, 256)
        return slab.at[j, r, w]

    def big_b(j, o, half):
        r = pl.ds(pl.multiple_of(c * 512 + o * 128, 128), 128)
        w = slice(None) if half is None else pl.ds(half * 256, 256)
        return slab.at[j, r, w]

    ax = Ring(NX, x, x_dev, small_a, lambda i: ax_s.at[i], lambda i: ax_r.at[i])
    by = Ring(NY, y, y_dev, small_b, lambda i: by_s.at[i], lambda i: by_r.at[i])
    ay = [Ring(NY, y, y_dev, functools.partial(big_a, 5 - s),
               lambda i, s=s: ay_s.at[s, i], lambda i, s=s: ay_r.at[s, i]) for s in range(3)]
    bx = [Ring(NX, x, x_dev, functools.partial(big_b, s),
               lambda i, s=s: bx_s.at[s, i], lambda i, s=s: bx_r.at[s, i]) for s in range(3)]

    to_sib = []

    def share(j, ref):
        i = sum(1 for jj, _ in to_sib if jj == j)
        cp = pltpu.make_async_remote_copy(
            src_ref=ref, dst_ref=ref, send_sem=dd_s.at[j, i], recv_sem=dd_r.at[j],
            device_id=(sib, t), device_id_type=MESH,
        )
        cp.start()
        to_sib.append((j, cp))

    def shared(j):
        half = slab.at[j, pl.ds(pl.multiple_of((1 - c) * 512, 512), 512), :]
        pltpu.make_async_remote_copy(
            src_ref=half, dst_ref=half, send_sem=dd_s.at[j, 0], recv_sem=dd_r.at[j],
            device_id=(sib, t), device_id_type=MESH,
        ).wait_recv()

    def big_step(ring, j, k):
        ring.wait(k)
        if k + 1 < ring.steps:
            ring.send(k + 1)
            for d in (0, 1):
                share(j, ring.region(ring.origin(d, k + 1), None))
        else:
            share(j, ring.region(ring.origin(0, k + 1), None))

    def multiply(j):
        part[j] = jnp.dot(cot_ref[...], slab[j], preferred_element_type=F32)

    def rs_copy(j, s):
        return pltpu.make_async_remote_copy(
            src_ref=snd.at[j], dst_ref=(fr_l if s > 0 else fr_r).at[j],
            send_sem=rs_s.at[j], recv_sem=(rl_r if s > 0 else rr_r).at[j],
            device_id=(f, t + s), device_id_type=MESH,
        )

    def rs_wait(j, s):
        ref, sem = (fr_l, rl_r) if s > 0 else (fr_r, rr_r)
        pltpu.make_async_remote_copy(
            src_ref=snd.at[j], dst_ref=ref.at[j], send_sem=rs_s.at[j], recv_sem=sem.at[j],
            device_id=(f, t), device_id_type=MESH,
        ).wait_recv()

    def slot(n):
        for s in (1, -1):
            for stage in range(3):
                hop = n - 2 * stage
                if not 0 <= hop < NT - 1:
                    continue
                at = hop if s > 0 else NT - 1 - hop
                dests = [j for j in (5 - stage, stage) if (j - at) * s > 0]
                if not dests:
                    continue

                @pl.when(t == at)
                def _():
                    for j in dests:
                        if hop > 0:
                            rs_wait(j, s)
                            snd[j] = (part[j] + (fr_l if s > 0 else fr_r)[j].astype(F32)).astype(BF16)
                        else:
                            snd[j] = part[j].astype(BF16)
                        rs_copy(j, s).start()

    def project(js):
        acc = None
        for j in js:
            d = lax.dot_general(att[j], slab[j], NT_DIMS, preferred_element_type=F32)
            acc = d if acc is None else acc + d
        return acc

    for j in range(NT):
        v = c * 32 + (y2 * 4 + x if j >= 3 else x * 8 + y2)
        mine = slab.at[j, pl.ds(pl.multiple_of(v * UNIT, UNIT), UNIT), :]
        pltpu.make_async_remote_copy(
            src_ref=mine, dst_ref=mine, send_sem=pre_s.at[0], recv_sem=pre_r.at[j],
            device_id=(f, t), device_id_type=MESH,
        ).wait_recv()

    ax.send(0)
    by.send(0)
    ax.wait(0)
    ax.send(1)
    by.wait(0)
    by.send(1)
    att_step(1)
    ax.wait(1)
    ay[0].send(0)
    ay[1].send(0)
    for s in range(3):
        share(5 - s, big_a(5 - s, y, None))
    by.wait(1)
    by.send(2)
    big_step(ay[0], 5, 0)
    by.wait(2)
    by.send(3)
    att_step(2)
    big_step(ay[1], 4, 0)
    by.wait(3)
    bx[0].send(0)
    bx[1].send(0)
    for s in range(3):
        share(s, big_b(s, x, None))
    big_step(ay[0], 5, 1)
    big_step(ay[1], 4, 1)
    big_step(bx[0], 0, 0)
    big_step(ay[0], 5, 2)
    att_step(3)
    big_step(bx[0], 0, 1)
    big_step(ay[1], 4, 2)
    ay[2].send(0)
    big_step(bx[1], 1, 0)
    bx[2].send(0)
    big_step(ay[0], 5, 3)
    shared(0)
    shared(5)
    multiply(5)
    multiply(0)
    slot(0)
    big_step(ay[2], 3, 0)
    big_step(bx[1], 1, 1)
    big_step(ay[1], 4, 3)
    att_step(4)
    slot(1)
    big_step(ay[2], 3, 1)
    big_step(bx[2], 2, 0)
    shared(1)
    shared(4)
    multiply(4)
    multiply(1)
    slot(2)
    big_step(ay[2], 3, 2)
    big_step(bx[2], 2, 1)
    slot(3)
    big_step(ay[2], 3, 3)
    shared(2)
    shared(3)
    multiply(3)
    multiply(2)
    slot(4)
    att_step(5)
    total = project((0, 1, 2))
    slot(5)
    total = total + project((3, 4, 5))
    proj_ref[...] = total.astype(BF16)
    slot(6)

    @pl.when(t > 0)
    def _():
        rs_wait(t, 1)
        part[t] += fr_l[t].astype(F32)

    @pl.when(t < NT - 1)
    def _():
        rs_wait(t, -1)
        part[t] += fr_r[t].astype(F32)

    for h in range(4):
        cols = slice(h * HD, (h + 1) * HD)
        qh, kh, vh = q_ref[:, cols], k_ref[:, cols], v_ref[:, cols]
        g = part[t, :, cols].astype(BF16)
        p = probs[h]
        gv_ref[:, cols] = lax.dot_general(p.astype(BF16), g, TN_DIMS, preferred_element_type=F32).astype(BF16)
        gp = lax.dot_general(g, vh, NT_DIMS, preferred_element_type=F32)
        delta = jnp.sum(gp * p, axis=-1, keepdims=True)
        gs = (p * (gp - delta) * SCALE).astype(BF16)
        gq_ref[:, cols] = jnp.dot(gs, kh, preferred_element_type=F32).astype(BF16)
        gk_ref[:, cols] = lax.dot_general(gs, qh, TN_DIMS, preferred_element_type=F32).astype(BF16)

    for i in range(3):
        for z in (0, 1):
            pre_copy(i, z).wait_send()
    for ring in [ax, by] + ay + bx:
        ring.finish()
    for _, cp in to_sib:
        cp.wait_send()
    for k in range(NT - 1):
        for s in (1, -1):
            has = (t >= k) if s > 0 else (t + k <= NT - 1)
            room = (t < NT - 1) if s > 0 else (t > 0)

            @pl.when(has & room)
            def _():
                att_copy(t - s * k, s, k).wait_send()
    for j in range(NT):
        @pl.when(t != j)
        def _():
            rs_copy(j, 1).wait_send()


def shards(queries, keys, values, out_weight, cotangent, image_ids):
    tok, width = queries.shape
    vmem = pl.BlockSpec(memory_space=pltpu.VMEM)
    dma = pltpu.SemaphoreType.DMA
    grads = jax.ShapeDtypeStruct((tok, width), BF16)
    return pl.pallas_call(
        kernel,
        out_shape=(jax.ShapeDtypeStruct(cotangent.shape, BF16), grads, grads, grads),
        in_specs=[vmem] * 6,
        out_specs=(vmem,) * 4,
        scratch_shapes=[
            pltpu.VMEM((NT, 1024, 512), BF16),
            pltpu.VMEM((NT, tok, width), BF16),
            pltpu.VMEM((NT, tok, width), BF16),
            pltpu.VMEM((NT, tok, width), BF16),
            pltpu.VMEM((NT, tok, width), BF16),
            pltpu.VMEM((NT, tok, width), F32),
            pltpu.VMEM((4, tok, tok), F32),
            dma((6,)), dma((6,)),
            dma((4,)), dma((4,)),
            dma((8,)), dma((8,)),
            dma((3, 8)), dma((3, 8)),
            dma((3, 4)), dma((3, 4)),
            dma((6, 8)), dma((6,)),
            dma((5,)), dma((5,)), dma((6,)),
            dma((6,)), dma((6,)), dma((6,)),
        ],
        compiler_params=pltpu.CompilerParams(
            collective_id=0, has_side_effects=True, vmem_limit_bytes=48 * 1024 * 1024
        ),
        name="attention",
    )(queries, keys, values, out_weight.T, cotangent, image_ids)


def solution(mesh):
    return jax.shard_map(
        shards,
        mesh=mesh,
        in_specs=(
            P("fsdp", "tensor"),
            P("fsdp", "tensor"),
            P("fsdp", "tensor"),
            P("tensor", "fsdp"),
            P("fsdp", "tensor"),
            P("fsdp", None),
        ),
        out_specs=(
            P("fsdp", "tensor"),
            P("fsdp", "tensor"),
            P("fsdp", "tensor"),
            P("fsdp", "tensor"),
        ),
        check_vma=False,
    )
```

```python
import functools

import jax
import jax.numpy as jnp
from jax import lax
from jax.experimental import pallas as pl
from jax.experimental.pallas import tpu as pltpu
from jax.sharding import PartitionSpec as P

HD = 128
HALF = 2 * HD
SCALE = HD ** (-0.5)
MESH = pl.DeviceIdType.MESH
NX, NY, NT = 4, 8, 6
UNIT = 16
F32 = jnp.float32
BF16 = jnp.bfloat16

NT_DIMS = (((1,), (1,)), ((), ()))
TN_DIMS = (((0,), (0,)), ((), ()))


def mod(a, n):
    return lax.rem(a + 4 * n, n)


def shift_of(slab):
    return 3 - slab % 3


def coords(f):
    return f // 16, (f // 4) % 4, (f // 2) % 2, f % 2


def index_of(y, x, zh, c):
    return ((y * NX + x) * 2 + zh) * 2 + c


class Ring:
    def __init__(self, n, pos, device, region, send_sem, recv_sem):
        self.n, self.pos, self.device, self.region = n, pos, device, region
        self.send_sem, self.recv_sem = send_sem, recv_sem
        self.steps = n // 2

    def copy(self, d, k, origin):
        last = k == self.steps - 1
        ref = self.region(origin, d if last else None)
        i = d * self.steps + k
        return pltpu.make_async_remote_copy(
            src_ref=ref, dst_ref=ref,
            send_sem=self.send_sem(i), recv_sem=self.recv_sem(i),
            device_id=self.device(1 if d == 0 else -1), device_id_type=MESH,
        )

    def origin(self, d, k):
        return mod(self.pos - k if d == 0 else self.pos + k, self.n)

    def send(self, k):
        for d in (0, 1):
            self.copy(d, k, self.origin(d, k)).start()

    def wait(self, k):
        for d in (0, 1):
            self.copy(d, k, self.origin(d, k + 1)).wait_recv()

    def finish(self):
        for k in range(self.steps):
            for d in (0, 1):
                self.copy(d, k, self.origin(d, k)).wait_send()


def kernel(q_hbm, k_hbm, v_hbm, wt_ref, cot_hbm, ids_hbm,
           proj_hbm, gq_hbm, gk_hbm, gv_hbm,
           proj_ref, gq_ref, gk_ref, gv_ref, q_ref, k_ref, v_ref, cot_ref, ids_ref,
           slab, att, fr, snd, part, probs, in_sem, out_sem,
           pre_s, pre_r, ax_s, ax_r, by_s, by_r, ay_s, ay_r, bx_s, bx_r,
           dd_s, dd_r, zr_s, zl_s, za_r, rs_s, rs_r):
    f = lax.axis_index("fsdp")
    t = lax.axis_index("tensor")
    y, x, zh, c = coords(f)
    turn = shift_of(t)
    y2 = lax.rem(y + turn, NY)
    x2 = lax.rem(x + turn, NX)
    in_a = t // 3

    sib = f + 1 - 2 * c
    x_dev = lambda s: (index_of(y, mod(x + s, NX), zh, c), t)
    y_dev = lambda s: (index_of(mod(y + s, NY), x, zh, c), t)

    loads = [
        pltpu.make_async_copy(src, dst, in_sem.at[i])
        for i, (src, dst) in enumerate((
            (ids_hbm, ids_ref), (q_hbm, q_ref), (k_hbm, k_ref), (v_hbm, v_ref), (cot_hbm, cot_ref)))
    ]
    for load in loads:
        load.start()

    barrier = pltpu.get_barrier_semaphore()

    def greet(device):
        pl.semaphore_signal(barrier, inc=1, device_id=device, device_id_type=MESH)

    def units(j):
        if j >= 3:
            return [c * 32 + y2 * 4 + x2]
        return [c * 32 + x2 * 8 + y2, c * 32 + x2 * 8 + lax.rem(y2 + 4, NY)]

    for j in range(NT):
        for v in units(j):
            greet(((64 * t + v) // 3, j))
    for s in (1, -1, 2):
        greet(x_dev(s))
    for s in (1, -1, 2, -2):
        greet(y_dev(s))
    greet((sib, t))

    @pl.when(t > 0)
    def _():
        greet((f, t - 1))

    @pl.when(t < NT - 1)
    def _():
        greet((f, t + 1))

    @pl.when((t == 3) | (t == 5))
    def _():
        greet((f, t - 2))

    @pl.when((t == 0) | (t == 2))
    def _():
        greet((f, t + 2))

    inner = ((t + NT - 1) // NT) * ((2 * NT - 2 - t) // NT)
    pl.semaphore_wait(barrier, 12 - 6 * in_a + 8 + 1 + 2 * inner)

    def pre_copy(i, z, h):
        u = 3 * f + i
        to = u // 64
        v = u % 64
        rest = v % 32
        ya, xa = rest // 4, rest % 4
        yb, xb = rest % 8, rest // 8
        yy = in_a * ya + (1 - in_a) * yb
        xx = in_a * xa + (1 - in_a) * xb
        yd = lax.rem(yy - shift_of(to) + 4 * h + NY, NY)
        xd = lax.rem(xx - shift_of(to) + NX, NX)
        return pltpu.make_async_remote_copy(
            src_ref=wt_ref.at[pl.ds(i * UNIT, UNIT), :],
            dst_ref=slab.at[t, pl.ds(pl.multiple_of(v * UNIT, UNIT), UNIT), :],
            send_sem=pre_s.at[(2 * i + z) * 2 + h], recv_sem=pre_r.at[h, t],
            device_id=(index_of(yd, xd, z, v // 32), to), device_id_type=MESH,
        )

    def pre_all(act):
        @pl.when(t < 3)
        def _():
            for i in range(3):
                for z in (0, 1):
                    for h in (0, 1):
                        act(pre_copy(i, z, h))

        @pl.when(t >= 3)
        def _():
            for i in range(3):
                for z in (0, 1):
                    act(pre_copy(i, z, 0))

    pre_all(lambda cp: cp.start())

    for load in loads:
        load.wait()

    ids_row = jnp.broadcast_to(ids_ref[...].astype(F32), (HD, HD))
    same = ids_row == ids_row.T
    for h in range(4):
        cols = slice(h * HD, (h + 1) * HD)
        s = lax.dot_general(q_ref[:, cols], k_ref[:, cols], NT_DIMS, preferred_element_type=F32) * SCALE
        s = jnp.where(same, s, -1e30)
        w = jnp.exp(s - jnp.max(s, axis=-1, keepdims=True))
        p = w / jnp.sum(w, axis=-1, keepdims=True)
        probs[h] = p
        a = jnp.dot(p.astype(BF16), v_ref[:, cols], preferred_element_type=F32)
        att[t, :, cols] = a.astype(BF16)

    def att_copy(block, s, k):
        return pltpu.make_async_remote_copy(
            src_ref=att.at[block], dst_ref=att.at[block],
            send_sem=(zr_s if s > 0 else zl_s).at[k], recv_sem=za_r.at[block],
            device_id=(f, t + s), device_id_type=MESH,
        )

    def att_wait(block):
        pltpu.make_async_remote_copy(
            src_ref=att.at[block], dst_ref=att.at[block],
            send_sem=zr_s.at[0], recv_sem=za_r.at[block],
            device_id=(f, t), device_id_type=MESH,
        ).wait_recv()

    def att_step(k):
        for s in (1, -1):
            block = t - s * k
            has = (t >= k) if s > 0 else (t + k <= NT - 1)
            room = (t < NT - 1) if s > 0 else (t > 0)
            if k > 0:
                @pl.when(has)
                def _():
                    att_wait(block)
            if k < NT - 1:
                @pl.when(has & room)
                def _():
                    att_copy(block, s, k).start()

    att_step(0)

    def small_a(o, half):
        r = pl.ds(pl.multiple_of(c * 512 + y2 * 64 + lax.rem(o + turn, NX) * UNIT, UNIT), UNIT)
        w = slice(None) if half is None else pl.ds(half * 256, 256)
        return slab.at[pl.ds(3, 3), r, w]

    def small_b(o, half):
        r = pl.ds(pl.multiple_of(c * 512 + x2 * 128 + lax.rem(o + turn, NY) * UNIT, UNIT), UNIT)
        w = slice(None) if half is None else pl.ds(half * 256, 256)
        return slab.at[pl.ds(0, 3), r, w]

    def big_a(j, o, half):
        r = pl.ds(pl.multiple_of(c * 512 + lax.rem(o + turn, NY) * 64, 64), 64)
        w = slice(None) if half is None else pl.ds(half * 256, 256)
        return slab.at[j, r, w]

    def big_b(j, o, half):
        r = pl.ds(pl.multiple_of(c * 512 + lax.rem(o + turn, NX) * 128, 128), 128)
        w = slice(None) if half is None else pl.ds(half * 256, 256)
        return slab.at[j, r, w]

    def sender(region, device, ssem, rsem):
        def copy(i, s, o, half):
            ref = region(o, half)
            return pltpu.make_async_remote_copy(
                src_ref=ref, dst_ref=ref, send_sem=ssem.at[i], recv_sem=rsem.at[i],
                device_id=device(s), device_id_type=MESH,
            )
        return copy

    ax = sender(small_a, x_dev, ax_s, ax_r)
    by = sender(small_b, y_dev, by_s, by_r)
    ax_plan = [(i, s, 0, None) for i, s in enumerate((1, -1, 2))]
    by_plan = [(0, 1, 0, None), (1, -1, 0, None), (2, 2, 0, None), (3, -2, 0, None), (4, 1, 4, None), (5, -1, 4, None)]

    def go(copy, pos, n, plan):
        for i, s, o, half in plan:
            copy(i, s, mod(pos + o, n), half).start()

    def come(copy, pos, n, plan):
        for i, s, o, half in plan:
            copy(i, s, mod(pos - s + o, n), half).wait_recv()

    def gone(copy, pos, n, plan):
        for i, s, o, half in plan:
            copy(i, s, mod(pos + o, n), half).wait_send()

    ay = [Ring(NY, y, y_dev, functools.partial(big_a, 5 - s),
               lambda i, s=s: ay_s.at[s, i], lambda i, s=s: ay_r.at[s, i]) for s in range(3)]
    bx = [Ring(NX, x, x_dev, functools.partial(big_b, s),
               lambda i, s=s: bx_s.at[s, i], lambda i, s=s: bx_r.at[s, i]) for s in range(3)]

    to_sib = []

    def share(j, ref):
        i = sum(1 for jj, _ in to_sib if jj == j)
        cp = pltpu.make_async_remote_copy(
            src_ref=ref, dst_ref=ref, send_sem=dd_s.at[j, i], recv_sem=dd_r.at[j],
            device_id=(sib, t), device_id_type=MESH,
        )
        cp.start()
        to_sib.append((j, cp))

    def shared(j):
        half = slab.at[j, pl.ds(pl.multiple_of((1 - c) * 512, 512), 512), :]
        pltpu.make_async_remote_copy(
            src_ref=half, dst_ref=half, send_sem=dd_s.at[j, 0], recv_sem=dd_r.at[j],
            device_id=(sib, t), device_id_type=MESH,
        ).wait_recv()

    def big_step(ring, j, k):
        ring.wait(k)
        if k + 1 < ring.steps:
            ring.send(k + 1)
            for d in (0, 1):
                share(j, ring.region(ring.origin(d, k + 1), None))
        else:
            share(j, ring.region(ring.origin(0, k + 1), None))

    def multiply(j):
        part[j] = jnp.dot(cot_ref[...], slab[j], preferred_element_type=F32)

    SIDES = (-1, -2, 1, 2)

    def rs_copy(j, s, b):
        i = SIDES.index(-s)
        cols = pl.ds(b * HALF, HALF)
        return pltpu.make_async_remote_copy(
            src_ref=snd.at[j, :, cols], dst_ref=fr.at[i, j, :, cols],
            send_sem=rs_s.at[b, j], recv_sem=rs_r.at[b, i, j],
            device_id=(f, t + s), device_id_type=MESH,
        )

    def rs_take(j, s, b):
        i = SIDES.index(s)
        cols = pl.ds(b * HALF, HALF)
        pltpu.make_async_remote_copy(
            src_ref=snd.at[j, :, cols], dst_ref=fr.at[i, j, :, cols],
            send_sem=rs_s.at[b, j], recv_sem=rs_r.at[b, i, j],
            device_id=(f, t), device_id_type=MESH,
        ).wait_recv()
        return fr[i, j, :, b * HALF:(b + 1) * HALF].astype(F32)

    def gather_in(j, takes, b):
        total = part[j, :, b * HALF:(b + 1) * HALF]
        for q in takes:
            total = total + rs_take(j, q, b)
        snd[j, :, b * HALF:(b + 1) * HALF] = total.astype(BF16)

    def step_of(at, j):
        flip = j < at
        a, d = (NT - 1 - at, NT - 1 - j) if flip else (at, j)
        takes, to = {
            0: ((), 1),
            1: ((-1,), 3 if d >= 3 else 2),
            2: ((), 3),
            3: ((-1, -2), 4 if d == 4 else 5),
            4: ((), 5),
        }[a]
        sign = -1 if flip else 1
        return tuple(sign * q for q in takes), sign * (to - a)

    def first(j):
        for at in range(NT):
            if at != j and not step_of(at, j)[0]:
                @pl.when(t == at)
                def _():
                    for b in (0, 1):
                        gather_in(j, (), b)
                        rs_copy(j, step_of(at, j)[1], b).start()

    def later(js):
        for at in range(NT):
            mine = [j for j in js if j != at and step_of(at, j)[0]]
            if mine:
                @pl.when(t == at)
                def _():
                    for j in mine:
                        takes, to = step_of(at, j)
                        for b in (0, 1):
                            gather_in(j, takes, b)
                            rs_copy(j, to, b).start()

    LAST = {0: (1, 2), 1: (-1, 1), 2: (-1, 1, 2), 3: (-1, -2, 1), 4: (-1, 1), 5: (-1, -2)}

    def last(b):
        for at in range(NT):
            @pl.when(t == at)
            def _():
                gather_in(at, LAST[at], b)

    def sent():
        for at in range(NT):
            @pl.when(t == at)
            def _():
                for j in range(NT):
                    if j != at:
                        for b in (0, 1):
                            rs_copy(j, step_of(at, j)[1], b).wait_send()

    def project(js):
        acc = None
        for j in js:
            d = lax.dot_general(att[j], slab[j], NT_DIMS, preferred_element_type=F32)
            acc = d if acc is None else acc + d
        return acc

    for j in range(NT):
        for h, v in enumerate(units(j)):
            mine = slab.at[j, pl.ds(pl.multiple_of(v * UNIT, UNIT), UNIT), :]
            pltpu.make_async_remote_copy(
                src_ref=mine, dst_ref=mine, send_sem=pre_s.at[0], recv_sem=pre_r.at[h, j],
                device_id=(f, t), device_id_type=MESH,
            ).wait_recv()

    go(ax, x, NX, ax_plan)
    go(by, y, NY, by_plan)
    att_step(1)
    come(ax, x, NX, ax_plan)
    for s in range(3):
        ay[s].send(0)
    come(by, y, NY, by_plan)
    for s in range(3):
        bx[s].send(0)
    for s in range(3):
        share(5 - s, big_a(5 - s, y, None))
    for s in range(3):
        share(s, big_b(s, x, None))
    att_step(2)
    for s in range(3):
        big_step(ay[s], 5 - s, 0)
    big_step(bx[0], 0, 0)
    big_step(ay[0], 5, 1)
    big_step(bx[1], 1, 0)
    big_step(ay[1], 4, 1)
    big_step(bx[2], 2, 0)
    big_step(ay[2], 3, 1)
    att_step(3)
    big_step(bx[0], 0, 1)
    big_step(ay[0], 5, 2)
    big_step(ay[1], 4, 2)
    big_step(ay[2], 3, 2)
    big_step(bx[1], 1, 1)
    shared(0)
    multiply(0)
    first(0)
    att_step(4)
    for s in range(3):
        big_step(ay[s], 5 - s, 3)
    big_step(bx[2], 2, 1)
    for j in (5, 1, 4, 3, 2):
        shared(j)
        multiply(j)
        first(j)

    pre_all(lambda cp: cp.wait_send())
    gone(ax, x, NX, ax_plan)
    gone(by, y, NY, by_plan)
    for ring in ay + bx:
        ring.finish()
    for _, cp in to_sib:
        cp.wait_send()

    later((0, 5))
    att_step(5)
    total = project((0, 1, 2))
    later((1, 4))
    total = total + project((3, 4, 5))
    proj_ref[...] = total.astype(BF16)
    stores = [
        pltpu.make_async_copy(src, dst, out_sem.at[i])
        for i, (src, dst) in enumerate((
            (proj_ref, proj_hbm), (gq_ref, gq_hbm), (gk_ref, gk_hbm), (gv_ref, gv_hbm)))
    ]
    stores[0].start()
    later((3, 2))

    for h in range(4):
        if h % 2 == 0:
            last(h // 2)
        cols = slice(h * HD, (h + 1) * HD)
        qh, kh, vh = q_ref[:, cols], k_ref[:, cols], v_ref[:, cols]
        g = snd[t, :, cols]
        p = probs[h]
        gv_ref[:, cols] = lax.dot_general(p.astype(BF16), g, TN_DIMS, preferred_element_type=F32).astype(BF16)
        gp = lax.dot_general(g, vh, NT_DIMS, preferred_element_type=F32)
        delta = jnp.sum(gp * p, axis=-1, keepdims=True)
        gs = (p * (gp - delta) * SCALE).astype(BF16)
        gq_ref[:, cols] = jnp.dot(gs, kh, preferred_element_type=F32).astype(BF16)
        gk_ref[:, cols] = lax.dot_general(gs, qh, TN_DIMS, preferred_element_type=F32).astype(BF16)
    for store in stores[1:]:
        store.start()

    for k in range(NT - 1):
        for s in (1, -1):
            has = (t >= k) if s > 0 else (t + k <= NT - 1)
            room = (t < NT - 1) if s > 0 else (t > 0)

            @pl.when(has & room)
            def _():
                att_copy(t - s * k, s, k).wait_send()
    sent()
    for store in stores:
        store.wait()


def hand_over(*refs):
    srcs, dsts, bufs, sems = refs[:4], refs[4:8], refs[8:12], refs[12]
    loads = [pltpu.make_async_copy(srcs[i], bufs[i], sems.at[0, i]) for i in range(4)]
    stores = [pltpu.make_async_copy(bufs[i], dsts[i], sems.at[1, i]) for i in range(4)]
    for load in loads:
        load.start()
    for load, store in zip(loads, stores):
        load.wait()
        store.start()
    for store in stores:
        store.wait()


def shards(queries, keys, values, out_weight, cotangent, image_ids):
    tok, width = queries.shape
    anywhere = pl.BlockSpec(memory_space=pl.ANY)
    dma = pltpu.SemaphoreType.DMA
    grads = jax.ShapeDtypeStruct((tok, width), BF16)
    outs = (jax.ShapeDtypeStruct(cotangent.shape, BF16), grads, grads, grads)
    results = pl.pallas_call(
        kernel,
        out_shape=outs,
        in_specs=[anywhere] * 6,
        out_specs=(anywhere,) * 4,
        scratch_shapes=[
            pltpu.VMEM(cotangent.shape, BF16),
            pltpu.VMEM((tok, width), BF16),
            pltpu.VMEM((tok, width), BF16),
            pltpu.VMEM((tok, width), BF16),
            pltpu.VMEM((tok, width), BF16),
            pltpu.VMEM((tok, width), BF16),
            pltpu.VMEM((tok, width), BF16),
            pltpu.VMEM(cotangent.shape, BF16),
            pltpu.VMEM(image_ids.shape, image_ids.dtype),
            pltpu.VMEM((NT, 1024, 512), BF16),
            pltpu.VMEM((NT, tok, width), BF16),
            pltpu.VMEM((4, NT, tok, width), BF16),
            pltpu.VMEM((NT, tok, width), BF16),
            pltpu.VMEM((NT, tok, width), F32),
            pltpu.VMEM((4, tok, tok), F32),
            dma((5,)), dma((4,)),
            dma((12,)), dma((2, 6)),
            dma((3,)), dma((3,)),
            dma((6,)), dma((6,)),
            dma((3, 8)), dma((3, 8)),
            dma((3, 4)), dma((3, 4)),
            dma((6, 8)), dma((6,)),
            dma((5,)), dma((5,)), dma((6,)),
            dma((2, 6)), dma((2, 4, 6)),
        ],
        compiler_params=pltpu.CompilerParams(
            collective_id=0, has_side_effects=True, vmem_limit_bytes=60 * 1024 * 1024
        ),
        name="attention",
    )(queries, keys, values, out_weight.T, cotangent, image_ids)
    return pl.pallas_call(
        hand_over,
        out_shape=outs,
        in_specs=[anywhere] * 4,
        out_specs=(anywhere,) * 4,
        scratch_shapes=[pltpu.VMEM(out.shape, BF16) for out in outs] + [dma((2, 4))],
        compiler_params=pltpu.CompilerParams(vmem_limit_bytes=60 * 1024 * 1024),
        name="hand_over",
    )(*results)


def solution(mesh):
    return jax.shard_map(
        shards,
        mesh=mesh,
        in_specs=(
            P("fsdp", "tensor"),
            P("fsdp", "tensor"),
            P("fsdp", "tensor"),
            P("tensor", "fsdp"),
            P("fsdp", "tensor"),
            P("fsdp", None),
        ),
        out_specs=(
            P("fsdp", "tensor"),
            P("fsdp", "tensor"),
            P("fsdp", "tensor"),
            P("fsdp", "tensor"),
        ),
        check_vma=False,
    )
```

```python
import functools

import jax
import jax.numpy as jnp
from jax import lax
from jax.experimental import pallas as pl
from jax.experimental.pallas import tpu as pltpu
from jax.sharding import PartitionSpec as P

HD = 128
HALF = 2 * HD
SCALE = HD ** (-0.5)
MESH = pl.DeviceIdType.MESH
NX, NY, NT = 4, 8, 6
UNIT = 16
AY, BX = (1, 3, 4), (0, 2, 5)
PLACE = (0, 3, 1, 4, 5, 2)
F32 = jnp.float32
BF16 = jnp.bfloat16

NT_DIMS = (((1,), (1,)), ((), ()))
TN_DIMS = (((0,), (0,)), ((), ()))


def mod(a, n):
    return lax.rem(a + 4 * n, n)


def shift_of(slab):
    return 3 - slab % 3


def coords(f):
    return f // 16, (f // 4) % 4, (f // 2) % 2, f % 2


def index_of(y, x, zh, c):
    return ((y * NX + x) * 2 + zh) * 2 + c


class Ring:
    def __init__(self, n, pos, device, region, send_sem, recv_sem):
        self.n, self.pos, self.device, self.region = n, pos, device, region
        self.send_sem, self.recv_sem = send_sem, recv_sem
        self.steps = n // 2

    def copy(self, d, k, origin):
        last = k == self.steps - 1
        ref = self.region(origin, d if last else None)
        i = d * self.steps + k
        return pltpu.make_async_remote_copy(
            src_ref=ref, dst_ref=ref,
            send_sem=self.send_sem(i), recv_sem=self.recv_sem(i),
            device_id=self.device(1 if d == 0 else -1), device_id_type=MESH,
        )

    def origin(self, d, k):
        return mod(self.pos - k if d == 0 else self.pos + k, self.n)

    def send(self, k):
        for d in (0, 1):
            self.copy(d, k, self.origin(d, k)).start()

    def wait(self, k):
        for d in (0, 1):
            self.copy(d, k, self.origin(d, k + 1)).wait_recv()

    def finish(self):
        for k in range(self.steps):
            for d in (0, 1):
                self.copy(d, k, self.origin(d, k)).wait_send()


def kernel(q_hbm, k_hbm, v_hbm, wt_ref, cot_hbm, ids_hbm,
           proj_hbm, gq_hbm, gk_hbm, gv_hbm,
           proj_ref, gq_ref, gk_ref, gv_ref, q_ref, k_ref, v_ref, cot_ref, ids_ref,
           slab, att, fr, snd, part, probs, in_sem, out_sem,
           pre_s, pre_r, ax_s, ax_r, by_s, by_r, ay_s, ay_r, bx_s, bx_r,
           dd_s, dd_r, zr_s, zl_s, za_r, rs_s, rs_r):
    f = lax.axis_index("fsdp")
    t = lax.axis_index("tensor")
    y, x, zh, c = coords(f)
    turn = shift_of(t)
    y2 = lax.rem(y + turn, NY)
    x2 = lax.rem(x + turn, NX)
    in_a = (t % 3) % 2 + (t // 3) * (1 - (t % 3 + 1) // 2)
    place = in_a * (t - t // 3 + 2) + (1 - in_a) * (t // 2)

    sib = f + 1 - 2 * c
    x_dev = lambda s: (index_of(y, mod(x + s, NX), zh, c), t)
    y_dev = lambda s: (index_of(mod(y + s, NY), x, zh, c), t)

    loads = [
        pltpu.make_async_copy(src, dst, in_sem.at[i])
        for i, (src, dst) in enumerate((
            (ids_hbm, ids_ref), (q_hbm, q_ref), (k_hbm, k_ref), (v_hbm, v_ref), (cot_hbm, cot_ref)))
    ]
    for load in loads:
        load.start()

    barrier = pltpu.get_barrier_semaphore()

    def greet(device):
        pl.semaphore_signal(barrier, inc=1, device_id=device, device_id_type=MESH)

    def units(j):
        if j in AY:
            return [c * 32 + y2 * 4 + x2]
        return [c * 32 + x2 * 8 + y2, c * 32 + x2 * 8 + lax.rem(y2 + 4, NY)]

    for j in range(NT):
        for v in units(j):
            greet(((64 * t + v) // 3, j))
    for s in (1, -1, 2):
        greet(x_dev(s))
    for s in (1, -1, 2, -2):
        greet(y_dev(s))
    greet((sib, t))

    @pl.when(t > 0)
    def _():
        greet((f, t - 1))

    @pl.when(t < NT - 1)
    def _():
        greet((f, t + 1))

    @pl.when((t == 3) | (t == 5))
    def _():
        greet((f, t - 2))

    @pl.when((t == 0) | (t == 2))
    def _():
        greet((f, t + 2))

    inner = ((t + NT - 1) // NT) * ((2 * NT - 2 - t) // NT)
    pl.semaphore_wait(barrier, 12 - 6 * in_a + 8 + 1 + 2 * inner)

    def pre_copy(i, z, h):
        u = 3 * f + i
        to = u // 64
        v = u % 64
        rest = v % 32
        ya, xa = rest // 4, rest % 4
        yb, xb = rest % 8, rest // 8
        yy = in_a * ya + (1 - in_a) * yb
        xx = in_a * xa + (1 - in_a) * xb
        yd = lax.rem(yy - shift_of(to) + 4 * h + NY, NY)
        xd = lax.rem(xx - shift_of(to) + NX, NX)
        return pltpu.make_async_remote_copy(
            src_ref=wt_ref.at[pl.ds(i * UNIT, UNIT), :],
            dst_ref=slab.at[place, pl.ds(pl.multiple_of(v * UNIT, UNIT), UNIT), :],
            send_sem=pre_s.at[(2 * i + z) * 2 + h], recv_sem=pre_r.at[h, t],
            device_id=(index_of(yd, xd, z, v // 32), to), device_id_type=MESH,
        )

    def pre_all(act):
        @pl.when(in_a == 0)
        def _():
            for i in range(3):
                for z in (0, 1):
                    for h in (0, 1):
                        act(pre_copy(i, z, h))

        @pl.when(in_a == 1)
        def _():
            for i in range(3):
                for z in (0, 1):
                    act(pre_copy(i, z, 0))

    pre_all(lambda cp: cp.start())

    for load in loads:
        load.wait()

    ids_row = jnp.broadcast_to(ids_ref[...].astype(F32), (HD, HD))
    same = ids_row == ids_row.T
    for h in range(4):
        cols = slice(h * HD, (h + 1) * HD)
        s = lax.dot_general(q_ref[:, cols], k_ref[:, cols], NT_DIMS, preferred_element_type=F32) * SCALE
        s = jnp.where(same, s, -1e30)
        w = jnp.exp(s - jnp.max(s, axis=-1, keepdims=True))
        p = w / jnp.sum(w, axis=-1, keepdims=True)
        probs[h] = p
        a = jnp.dot(p.astype(BF16), v_ref[:, cols], preferred_element_type=F32)
        att[t, :, cols] = a.astype(BF16)

    def att_copy(block, s, k):
        return pltpu.make_async_remote_copy(
            src_ref=att.at[block], dst_ref=att.at[block],
            send_sem=(zr_s if s > 0 else zl_s).at[k], recv_sem=za_r.at[block],
            device_id=(f, t + s), device_id_type=MESH,
        )

    def att_wait(block):
        pltpu.make_async_remote_copy(
            src_ref=att.at[block], dst_ref=att.at[block],
            send_sem=zr_s.at[0], recv_sem=za_r.at[block],
            device_id=(f, t), device_id_type=MESH,
        ).wait_recv()

    def att_step(k):
        for s in (1, -1):
            block = t - s * k
            has = (t >= k) if s > 0 else (t + k <= NT - 1)
            room = (t < NT - 1) if s > 0 else (t > 0)
            if k > 0:
                @pl.when(has)
                def _():
                    att_wait(block)
            if k < NT - 1:
                @pl.when(has & room)
                def _():
                    att_copy(block, s, k).start()

    att_step(0)

    def small_a(o, half):
        r = pl.ds(pl.multiple_of(c * 512 + y2 * 64 + lax.rem(o + turn, NX) * UNIT, UNIT), UNIT)
        w = slice(None) if half is None else pl.ds(half * 256, 256)
        return slab.at[pl.ds(3, 3), r, w]

    def small_b(o, half):
        r = pl.ds(pl.multiple_of(c * 512 + x2 * 128 + lax.rem(o + turn, NY) * UNIT, UNIT), UNIT)
        w = slice(None) if half is None else pl.ds(half * 256, 256)
        return slab.at[pl.ds(0, 3), r, w]

    def big_a(j, o, half):
        r = pl.ds(pl.multiple_of(c * 512 + lax.rem(o + turn, NY) * 64, 64), 64)
        w = slice(None) if half is None else pl.ds(half * 256, 256)
        return slab.at[PLACE[j], r, w]

    def big_b(j, o, half):
        r = pl.ds(pl.multiple_of(c * 512 + lax.rem(o + turn, NX) * 128, 128), 128)
        w = slice(None) if half is None else pl.ds(half * 256, 256)
        return slab.at[PLACE[j], r, w]

    def sender(region, device, ssem, rsem):
        def copy(i, s, o, half):
            ref = region(o, half)
            return pltpu.make_async_remote_copy(
                src_ref=ref, dst_ref=ref, send_sem=ssem.at[i], recv_sem=rsem.at[i],
                device_id=device(s), device_id_type=MESH,
            )
        return copy

    ax = sender(small_a, x_dev, ax_s, ax_r)
    by = sender(small_b, y_dev, by_s, by_r)
    ax_plan = [(i, s, 0, None) for i, s in enumerate((1, -1, 2))]
    by_plan = [(0, 1, 0, None), (1, -1, 0, None), (2, 2, 0, None), (3, -2, 0, None), (4, 1, 4, None), (5, -1, 4, None)]

    def go(copy, pos, n, plan):
        for i, s, o, half in plan:
            copy(i, s, mod(pos + o, n), half).start()

    def come(copy, pos, n, plan):
        for i, s, o, half in plan:
            copy(i, s, mod(pos - s + o, n), half).wait_recv()

    def gone(copy, pos, n, plan):
        for i, s, o, half in plan:
            copy(i, s, mod(pos + o, n), half).wait_send()

    ay = [Ring(NY, y, y_dev, functools.partial(big_a, AY[s]),
               lambda i, s=s: ay_s.at[s, i], lambda i, s=s: ay_r.at[s, i]) for s in range(3)]
    bx = [Ring(NX, x, x_dev, functools.partial(big_b, BX[s]),
               lambda i, s=s: bx_s.at[s, i], lambda i, s=s: bx_r.at[s, i]) for s in range(3)]

    to_sib = []

    def share(j, ref):
        i = sum(1 for jj, _ in to_sib if jj == j)
        cp = pltpu.make_async_remote_copy(
            src_ref=ref, dst_ref=ref, send_sem=dd_s.at[j, i], recv_sem=dd_r.at[j],
            device_id=(sib, t), device_id_type=MESH,
        )
        cp.start()
        to_sib.append((j, cp))

    def shared(j):
        half = slab.at[PLACE[j], pl.ds(pl.multiple_of((1 - c) * 512, 512), 512), :]
        pltpu.make_async_remote_copy(
            src_ref=half, dst_ref=half, send_sem=dd_s.at[j, 0], recv_sem=dd_r.at[j],
            device_id=(sib, t), device_id_type=MESH,
        ).wait_recv()

    def big_step(ring, j, k):
        ring.wait(k)
        if k + 1 < ring.steps:
            ring.send(k + 1)
            for d in (0, 1):
                share(j, ring.region(ring.origin(d, k + 1), None))
        else:
            share(j, ring.region(ring.origin(0, k + 1), None))

    def multiply(j):
        part[j] = jnp.dot(cot_ref[...], slab[PLACE[j]], preferred_element_type=F32)

    SIDES = (-1, -2, 1, 2)

    def rs_copy(j, s, b):
        i = SIDES.index(-s)
        cols = pl.ds(b * HALF, HALF)
        return pltpu.make_async_remote_copy(
            src_ref=snd.at[j, :, cols], dst_ref=fr.at[i, j, :, cols],
            send_sem=rs_s.at[b, j], recv_sem=rs_r.at[b, i, j],
            device_id=(f, t + s), device_id_type=MESH,
        )

    def rs_take(j, s, b):
        i = SIDES.index(s)
        cols = pl.ds(b * HALF, HALF)
        pltpu.make_async_remote_copy(
            src_ref=snd.at[j, :, cols], dst_ref=fr.at[i, j, :, cols],
            send_sem=rs_s.at[b, j], recv_sem=rs_r.at[b, i, j],
            device_id=(f, t), device_id_type=MESH,
        ).wait_recv()
        return fr[i, j, :, b * HALF:(b + 1) * HALF].astype(F32)

    def gather_in(j, takes, b):
        total = part[j, :, b * HALF:(b + 1) * HALF]
        for q in takes:
            total = total + rs_take(j, q, b)
        snd[j, :, b * HALF:(b + 1) * HALF] = total.astype(BF16)

    def step_of(at, j):
        flip = j < at
        a, d = (NT - 1 - at, NT - 1 - j) if flip else (at, j)
        takes, to = {
            0: ((), 1),
            1: ((-1,), 3 if d >= 3 else 2),
            2: ((), 3),
            3: ((-1, -2), 4 if d == 4 else 5),
            4: ((), 5),
        }[a]
        sign = -1 if flip else 1
        return tuple(sign * q for q in takes), sign * (to - a)

    def first(j):
        for at in range(NT):
            if at != j and not step_of(at, j)[0]:
                @pl.when(t == at)
                def _():
                    for b in (0, 1):
                        gather_in(j, (), b)
                        rs_copy(j, step_of(at, j)[1], b).start()

    def later(js):
        for at in range(NT):
            mine = [j for j in js if j != at and step_of(at, j)[0]]
            if mine:
                @pl.when(t == at)
                def _():
                    for j in mine:
                        takes, to = step_of(at, j)
                        for b in (0, 1):
                            gather_in(j, takes, b)
                            rs_copy(j, to, b).start()

    LAST = {0: (1, 2), 1: (-1, 1), 2: (-1, 1, 2), 3: (-1, -2, 1), 4: (-1, 1), 5: (-1, -2)}

    def last(b):
        for at in range(NT):
            @pl.when(t == at)
            def _():
                gather_in(at, LAST[at], b)

    def sent():
        for at in range(NT):
            @pl.when(t == at)
            def _():
                for j in range(NT):
                    if j != at:
                        for b in (0, 1):
                            rs_copy(j, step_of(at, j)[1], b).wait_send()

    def project(js):
        acc = None
        for j in js:
            d = lax.dot_general(att[j], slab[PLACE[j]], NT_DIMS, preferred_element_type=F32)
            acc = d if acc is None else acc + d
        return acc

    for j in range(NT):
        for h, v in enumerate(units(j)):
            mine = slab.at[PLACE[j], pl.ds(pl.multiple_of(v * UNIT, UNIT), UNIT), :]
            pltpu.make_async_remote_copy(
                src_ref=mine, dst_ref=mine, send_sem=pre_s.at[0], recv_sem=pre_r.at[h, j],
                device_id=(f, t), device_id_type=MESH,
            ).wait_recv()

    go(ax, x, NX, ax_plan)
    go(by, y, NY, by_plan)
    att_step(1)
    come(ax, x, NX, ax_plan)
    for s in range(3):
        ay[s].send(0)
    come(by, y, NY, by_plan)
    bx[0].send(0)
    bx[1].send(0)
    for j in AY:
        share(j, big_a(j, y, None))
    for j in BX:
        share(j, big_b(j, x, None))
    att_step(2)

    def step_a(s, k):
        big_step(ay[s], AY[s], k)

    def step_b(s, k):
        big_step(bx[s], BX[s], k)

    def finish(j):
        shared(j)
        multiply(j)
        first(j)

    step_a(0, 0)
    step_b(0, 0)
    step_a(1, 0)
    step_a(2, 0)
    step_b(1, 0)
    bx[2].send(0)
    step_a(0, 1)
    step_b(0, 1)
    step_a(1, 1)
    att_step(3)
    step_a(2, 1)
    finish(BX[0])
    step_b(1, 1)
    step_a(0, 2)
    step_a(1, 2)
    step_b(2, 0)
    step_a(2, 2)
    finish(BX[1])
    att_step(4)
    for s in range(3):
        step_a(s, 3)
    step_b(2, 1)
    finish(AY[0])
    finish(AY[1])
    finish(AY[2])
    finish(BX[2])
    later(BX[:2])
    later((1, 3))
    later((4, 5))

    att_step(5)
    proj_ref[...] = (project((0, 1, 2)) + project((3, 4, 5))).astype(BF16)
    stores = [
        pltpu.make_async_copy(src, dst, out_sem.at[i])
        for i, (src, dst) in enumerate((
            (proj_ref, proj_hbm), (gq_ref, gq_hbm), (gk_ref, gk_hbm), (gv_ref, gv_hbm)))
    ]
    stores[0].start()

    pre_all(lambda cp: cp.wait_send())
    gone(ax, x, NX, ax_plan)
    gone(by, y, NY, by_plan)
    for ring in ay + bx:
        ring.finish()
    for _, cp in to_sib:
        cp.wait_send()

    for h in range(4):
        if h % 2 == 0:
            last(h // 2)
        cols = slice(h * HD, (h + 1) * HD)
        qh, kh, vh = q_ref[:, cols], k_ref[:, cols], v_ref[:, cols]
        g = snd[t, :, cols]
        p = probs[h]
        gv_ref[:, cols] = lax.dot_general(p.astype(BF16), g, TN_DIMS, preferred_element_type=F32).astype(BF16)
        gp = lax.dot_general(g, vh, NT_DIMS, preferred_element_type=F32)
        delta = jnp.sum(gp * p, axis=-1, keepdims=True)
        gs = (p * (gp - delta) * SCALE).astype(BF16)
        gq_ref[:, cols] = jnp.dot(gs, kh, preferred_element_type=F32).astype(BF16)
        gk_ref[:, cols] = lax.dot_general(gs, qh, TN_DIMS, preferred_element_type=F32).astype(BF16)
    for store in stores[1:]:
        store.start()

    for k in range(NT - 1):
        for s in (1, -1):
            has = (t >= k) if s > 0 else (t + k <= NT - 1)
            room = (t < NT - 1) if s > 0 else (t > 0)

            @pl.when(has & room)
            def _():
                att_copy(t - s * k, s, k).wait_send()
    sent()
    for store in stores:
        store.wait()


def hand_over(*refs):
    srcs, dsts, bufs, sems = refs[:4], refs[4:8], refs[8:12], refs[12]
    loads = [pltpu.make_async_copy(srcs[i], bufs[i], sems.at[0, i]) for i in range(4)]
    stores = [pltpu.make_async_copy(bufs[i], dsts[i], sems.at[1, i]) for i in range(4)]
    for load in loads:
        load.start()
    for load, store in zip(loads, stores):
        load.wait()
        store.start()
    for store in stores:
        store.wait()


def shards(queries, keys, values, out_weight, cotangent, image_ids):
    tok, width = queries.shape
    anywhere = pl.BlockSpec(memory_space=pl.ANY)
    dma = pltpu.SemaphoreType.DMA
    grads = jax.ShapeDtypeStruct((tok, width), BF16)
    outs = (jax.ShapeDtypeStruct(cotangent.shape, BF16), grads, grads, grads)
    results = pl.pallas_call(
        kernel,
        out_shape=outs,
        in_specs=[anywhere] * 6,
        out_specs=(anywhere,) * 4,
        scratch_shapes=[
            pltpu.VMEM(cotangent.shape, BF16),
            pltpu.VMEM((tok, width), BF16),
            pltpu.VMEM((tok, width), BF16),
            pltpu.VMEM((tok, width), BF16),
            pltpu.VMEM((tok, width), BF16),
            pltpu.VMEM((tok, width), BF16),
            pltpu.VMEM((tok, width), BF16),
            pltpu.VMEM(cotangent.shape, BF16),
            pltpu.VMEM(image_ids.shape, image_ids.dtype),
            pltpu.VMEM((NT, 1024, 512), BF16),
            pltpu.VMEM((NT, tok, width), BF16),
            pltpu.VMEM((4, NT, tok, width), BF16),
            pltpu.VMEM((NT, tok, width), BF16),
            pltpu.VMEM((NT, tok, width), F32),
            pltpu.VMEM((4, tok, tok), F32),
            dma((5,)), dma((4,)),
            dma((12,)), dma((2, 6)),
            dma((3,)), dma((3,)),
            dma((6,)), dma((6,)),
            dma((3, 8)), dma((3, 8)),
            dma((3, 4)), dma((3, 4)),
            dma((6, 8)), dma((6,)),
            dma((5,)), dma((5,)), dma((6,)),
            dma((2, 6)), dma((2, 4, 6)),
        ],
        compiler_params=pltpu.CompilerParams(
            collective_id=0, has_side_effects=True, vmem_limit_bytes=60 * 1024 * 1024
        ),
        name="attention",
    )(queries, keys, values, out_weight.T, cotangent, image_ids)
    return pl.pallas_call(
        hand_over,
        out_shape=outs,
        in_specs=[anywhere] * 4,
        out_specs=(anywhere,) * 4,
        scratch_shapes=[pltpu.VMEM(out.shape, BF16) for out in outs] + [dma((2, 4))],
        compiler_params=pltpu.CompilerParams(vmem_limit_bytes=60 * 1024 * 1024),
        name="hand_over",
    )(*results)


def solution(mesh):
    return jax.shard_map(
        shards,
        mesh=mesh,
        in_specs=(
            P("fsdp", "tensor"),
            P("fsdp", "tensor"),
            P("fsdp", "tensor"),
            P("tensor", "fsdp"),
            P("fsdp", "tensor"),
            P("fsdp", None),
        ),
        out_specs=(
            P("fsdp", "tensor"),
            P("fsdp", "tensor"),
            P("fsdp", "tensor"),
            P("fsdp", "tensor"),
        ),
        check_vma=False,
    )
```
